32 devices in a mesh: lon: 8 (over z, y), band: 4 (over x, core).
Axes of the slice: x: 2, y: 2, z: 4, core: 2. Of those that a mesh axis runs over, the one named last changes fastest.
Arguments:
- denoised_tokens: bfloat16 [4, 32, 1920], P('band', 'lon'), may hold values from -6 to 6
- sequence_row_index: int32 [4, 32], P('band'), may hold values from 0 to 31, each once within a row
- latent_frame_cache: bfloat16 [4, 128, 1920], P(None, 'band', 'lon'), may hold values from -6 to 6
- cache_slot_order: int32 [4], replicated, may hold values from 0 to 3, each once
- temporal_taps_weight: bfloat16 [3, 16, 16], replicated, may hold values from -0.875 to 0.875
- input_weight: bfloat16 [9, 16, 256], replicated, may hold values from -0.5 to 0.5
- latent_conv_weights: bfloat16 [2, 9, 256, 256], replicated, may hold values from -0.125 to 0.125
- upsampled_weight: bfloat16 [9, 256, 256], replicated, may hold values from -0.125 to 0.125
- upper_conv_weights: bfloat16 [2, 9, 256, 256], replicated, may hold values from -0.125 to 0.125
- latent_norm_gains: float32 [2, 256], replicated, may hold values from 0.5 to 1.5
- upper_norm_gains: float32 [2, 256], replicated, may hold values from 0.5 to 1.5
Outputs:
- decoded: bfloat16 [256, 240, 256], P('band', 'lon')
The draws below stay inside these ranges and needn't reach their ends.
Inputs may be any that keep to these rules, and one draw needn't show every extreme that they name: Each row sequence_row_index[b] holds every position 0..31 once. cache_slot_order holds each slot once.
All inputs are finite; a program needn't handle non-finite values.
Results may differ from the reference program's by a relative error of at most 0.02.
Values may be sent and summed in bfloat16 or wider, within the bound.
A program may use at most 128 MiB of HBM per device.

```python
import jax
import jax.numpy as jnp
from jax import lax

LATENT_CHANNELS = 16
CH = 256
CACHE = 4
BAND_HEIGHT = 32
H = 128
PANORAMA_WIDTH = 120
N_BAND = 4


def levels(key, extent, cuts, smallest, largest):
    def one(axis_at, blocks):
        heights = jax.random.uniform(jax.random.fold_in(jax.random.fold_in(key, 6), axis_at), (blocks,), jnp.float32, smallest / len(cuts), largest / len(cuts))
        return jnp.repeat(jnp.exp(heights), extent[axis_at] // blocks).reshape((-1,) + (1,) * (len(extent) - axis_at - 1))

    loudness = one(*cuts[0])
    for cut in cuts[1:]:
        loudness = loudness * one(*cut)
    return loudness


def centred(key, shape, deviation, most, pieces=(), kind=jnp.bfloat16):
    array = jax.random.normal(key, shape, jnp.float32) * deviation
    if len(pieces) > 0:
        array = levels(key, shape, pieces, -0.22, 0.18) * array
    return jnp.clip(array, min=-most, max=most).astype(kind)


def setup_inputs(seed: int = 0) -> dict:
    key_of = jax.random.split(jax.random.key(seed), 12)
    return {
        "denoised_tokens": centred(key_of[0], (N_BAND, BAND_HEIGHT, PANORAMA_WIDTH * LATENT_CHANNELS), 1.0, 6.0, ((0, 4), (1, 8))),
        "sequence_row_index": jax.vmap(lambda own: jax.random.permutation(own, BAND_HEIGHT))(jax.random.split(key_of[1], N_BAND)).reshape((N_BAND, BAND_HEIGHT)).astype(jnp.int32),
        "latent_frame_cache": centred(key_of[2], (CACHE, H, PANORAMA_WIDTH * LATENT_CHANNELS), 1.0, 6.0, ((1, 4), (2, 8))),
        "cache_slot_order": jax.random.permutation(key_of[3], CACHE).astype(jnp.int32),
        "temporal_taps_weight": centred(key_of[4], (3, LATENT_CHANNELS, LATENT_CHANNELS), (3 * LATENT_CHANNELS) ** -0.5, 0.875),
        "input_weight": centred(key_of[5], (9, LATENT_CHANNELS, CH), (9 * LATENT_CHANNELS) ** -0.5, 0.5),
        "latent_conv_weights": centred(key_of[6], (2, 9, CH, CH), (9 * CH) ** -0.5, 0.125),
        "upsampled_weight": centred(key_of[7], (9, CH, CH), (9 * CH) ** -0.5, 0.125),
        "upper_conv_weights": centred(key_of[8], (2, 9, CH, CH), (9 * CH) ** -0.5, 0.125),
        "latent_norm_gains": jnp.clip(jax.random.uniform(key_of[9], (2, CH), jnp.float32, 0.5, 1.5), 0.5, 1.5),
        "upper_norm_gains": jnp.clip(jax.random.uniform(key_of[10], (2, CH), jnp.float32, 0.5, 1.5), 0.5, 1.5),
    }


def activate(activity, gain_row):
    values = activity.astype(jnp.float32)
    scaled = values * jax.lax.rsqrt(lax.optimization_barrier(jnp.mean(values * values, axis=-1, keepdims=True)) + 1e-06) * gain_row
    return jax.nn.silu(scaled).astype(jnp.bfloat16)

def conv_valid(padded, weight):
    row_count = padded.shape[0] - 2
    col_count = padded.shape[1] - 2
    inputs = padded.shape[2]
    summed = jnp.zeros((row_count * col_count, weight.shape[2]), jnp.float32)
    for offset in range(9):
        shift_row = offset // 3
        shift_col = offset % 3
        window = padded[shift_row:shift_row + row_count, shift_col:shift_col + col_count].reshape(row_count * col_count, inputs)
        summed = summed + jnp.dot(window, weight[offset], preferred_element_type=jnp.float32)
    return summed.reshape(row_count, col_count, weight.shape[2])

def pad_sphere(activity):
    beside_all = jnp.concatenate([activity[:, -1:], activity, activity[:, :1]], axis=1)
    border = jnp.zeros((1,) + beside_all.shape[1:], activity.dtype)
    return jnp.concatenate([border, beside_all, border], axis=0)

def conv_full(activity, weight):
    return conv_valid(pad_sphere(activity), weight)

def res_block(activity, gain_rows, weights):
    inner_sum = conv_full(activate(activity, gain_rows[0]), weights[0])
    branch = conv_full(activate(inner_sum, gain_rows[1]), weights[1])
    return (activity.astype(jnp.float32) + branch).astype(jnp.bfloat16)

def reference(denoised_tokens, sequence_row_index, latent_frame_cache, cache_slot_order, temporal_taps_weight, input_weight, latent_conv_weights, upsampled_weight, upper_conv_weights, latent_norm_gains, upper_norm_gains):
    sorted_rows = jax.vmap(lambda token_rows, row_places: token_rows[row_places])(denoised_tokens, sequence_row_index)
    latent = sorted_rows.reshape(H * PANORAMA_WIDTH, LATENT_CHANNELS)
    newest = latent_frame_cache[cache_slot_order[0]].reshape(H * PANORAMA_WIDTH, LATENT_CHANNELS)
    oldest = latent_frame_cache[cache_slot_order[1]].reshape(H * PANORAMA_WIDTH, LATENT_CHANNELS)
    mixture = jnp.dot(latent, temporal_taps_weight[0], preferred_element_type=jnp.float32)
    mixture = mixture + jnp.dot(newest, temporal_taps_weight[1], preferred_element_type=jnp.float32)
    mixture = mixture + jnp.dot(oldest, temporal_taps_weight[2], preferred_element_type=jnp.float32)
    temporal = mixture.astype(jnp.bfloat16).reshape(H, PANORAMA_WIDTH, LATENT_CHANNELS)
    opening = conv_full(temporal, input_weight).astype(jnp.bfloat16)
    low_res = res_block(opening, latent_norm_gains, latent_conv_weights)
    upsampled = jnp.repeat(jnp.repeat(low_res, 2, axis=0), 2, axis=1)
    high_res = conv_full(upsampled, upsampled_weight).astype(jnp.bfloat16)
    return res_block(high_res, upper_norm_gains, upper_conv_weights)
```

```python
import functools

import jax
import jax.numpy as jnp
from jax import lax
from jax.experimental import pallas as pl
from jax.experimental.pallas import tpu as pltpu
from jax.sharding import PartitionSpec as P

HALO = 5
F32 = jnp.float32
BF16 = jnp.bfloat16


def round_up(value, step):
    return (value + step - 1) // step * step


def tile_of(rows, pitch, even=False):
    best = 2 if even else 1
    for count in range(1, rows + 1):
        if rows % count == 0 and count * pitch <= 640 and not (even and count % 2):
            best = count
    return best


def activate(values, gain):
    scale = lax.rsqrt(jnp.mean(values * values, axis=-1, keepdims=True) + 1e-06)
    half = values * scale * (gain * 0.5)
    return half + half * jnp.tanh(half)


def roll_up(values, count):
    return pltpu.roll(values, values.shape[0] - count, 0)


def decoder_kernel(
    dims,
    band_ref,
    patches_ref,
    first_ref,
    low_w_ref,
    up_w_ref,
    high_w_ref,
    low_gain_ref,
    high_gain_ref,
    out_ref,
    opening,
    low_a,
    low_b,
    low_res,
    phase_w,
    field,
    high_a,
    high_b,
    weave,
):
    rows, cols, pitch, narrow, bands = dims
    ch = out_ref.shape[-1]
    band = band_ref[0]
    at_top = band == 0
    at_bottom = band == bands - 1

    def blank(ref, lead, row_slice):
        shape = ref.at[lead, row_slice].shape if lead is not None else ref.at[row_slice].shape
        if lead is None:
            ref[row_slice] = jnp.zeros(shape, ref.dtype)
        else:
            ref[lead, row_slice] = jnp.zeros(shape, ref.dtype)

    def blank_ends(ref, copies, top, bottom):
        total = ref.shape[1]

        @pl.when(at_top)
        def _():
            for k in range(copies):
                blank(ref, k, pl.ds(0, top))

        @pl.when(at_bottom)
        def _():
            for k in range(copies):
                blank(ref, k, pl.ds(total - bottom, bottom))

    total = rows + 8
    tile = tile_of(total, pitch)

    @pl.loop(0, total // tile)
    def _(step):
        start = step * tile
        part = patches_ref[pl.ds(start, tile)].reshape(tile * pitch, -1)
        summed = jnp.dot(part, first_ref[...], preferred_element_type=F32)
        summed = summed.astype(BF16).astype(F32)
        shape = (tile, pitch, ch)
        opening[pl.ds(start, tile)] = roll_up(summed, 2).astype(BF16).reshape(shape)
        active = activate(summed, low_gain_ref[0:1])
        low_a[0, pl.ds(start, tile)] = active.astype(BF16).reshape(shape)
        low_a[1, pl.ds(start, tile)] = roll_up(active, 1).astype(BF16).reshape(shape)
        low_a[2, pl.ds(start, tile)] = roll_up(active, 2).astype(BF16).reshape(shape)

    blank_ends(low_a, 3, 4, 4)

    def low_conv(source, start, tile, which):
        parts = []
        for p in range(3):
            for q in range(3):
                part = source[q, pl.ds(start + p, tile)]
                parts.append(part.reshape(tile * pitch, ch))
        return jnp.dot(
            jnp.concatenate(parts, axis=1), low_w_ref[which], preferred_element_type=F32
        )

    total = rows + 6
    tile = tile_of(total, pitch)

    @pl.loop(0, total // tile)
    def _(step):
        start = step * tile
        shape = (tile, pitch, ch)
        active = activate(low_conv(low_a, start, tile, 0), low_gain_ref[1:2])
        low_b[0, pl.ds(start, tile)] = active.astype(BF16).reshape(shape)
        low_b[1, pl.ds(start, tile)] = roll_up(active, 1).astype(BF16).reshape(shape)
        low_b[2, pl.ds(start, tile)] = roll_up(active, 2).astype(BF16).reshape(shape)

    blank_ends(low_b, 3, 3, 3)

    total = rows + 4
    tile = tile_of(total, pitch)

    @pl.loop(0, total // tile)
    def _(step):
        start = step * tile
        shape = (tile, pitch, ch)
        summed = low_conv(low_b, start, tile, 1)
        summed = summed + opening[pl.ds(start + 2, tile)].reshape(tile * pitch, ch).astype(F32)
        for shift in range(4):
            moved = summed if shift == 0 else roll_up(summed, shift)
            low_res[shift, pl.ds(start, tile)] = moved.astype(BF16).reshape(shape)[:, :narrow]

    blank_ends(low_res, 4, 2, 2)

    def tap(p, q):
        return up_w_ref[3 * p + q].astype(F32)

    groups = (((0,), (1, 2)), ((0, 1), (2,)))
    for a in range(2):
        for b in range(2):
            for p in range(2):
                for q in range(2):
                    summed = None
                    for pp in groups[a][p]:
                        for qq in groups[b][q]:
                            term = tap(pp, qq)
                            summed = term if summed is None else summed + term
                    base = (2 * p + q) * ch
                    phase_w[a, pl.ds(base, ch), pl.ds(b * ch, ch)] = summed.astype(BF16)

    total = rows + 2
    tile = tile_of(total, narrow)

    @pl.loop(0, total // tile)
    def _(step):
        start = step * tile
        shape = (tile, narrow, ch)
        for a in range(2):

            def up_conv(left, low_n, high_n):
                parts = []
                for p in range(2):
                    for q in range(2):
                        part = low_res[left + q, pl.ds(start + a + p, tile)]
                        parts.append(part.reshape(tile * narrow, ch))
                return jnp.dot(
                    jnp.concatenate(parts, axis=1),
                    phase_w[a, :, low_n:high_n],
                    preferred_element_type=F32,
                )

            def keep(slot, summed, kept):
                rounded = summed.astype(BF16)
                if kept is not None:
                    field[kept, pl.ds(start, tile), a] = rounded.reshape(shape)
                active = activate(rounded.astype(F32), high_gain_ref[0:1])
                high_a[slot, pl.ds(start, tile), a] = active.astype(BF16).reshape(shape)

            both = up_conv(1, 0, 2 * ch)
            keep(0, both[:, :ch], 0)
            keep(2, both[:, ch:], None)
            keep(1, up_conv(0, 0, ch), None)
            keep(3, up_conv(2, ch, 2 * ch), 1)

    blank_ends(high_a, 4, 1, 1)

    def high_conv(source, slots, start, tile, which):
        parts = []
        views = [
            source[s, pl.ds(start, tile // 2 + 1)].reshape(tile + 2, narrow, ch) for s in slots
        ]
        for p in range(3):
            for q in range(3):
                parts.append(views[q][p : p + tile].reshape(tile * narrow, ch))
        return jnp.dot(
            jnp.concatenate(parts, axis=1), high_w_ref[which], preferred_element_type=F32
        )

    total = 2 * rows + 2
    tile = tile_of(total, narrow, True)

    @pl.loop(0, total // tile)
    def _(step):
        half = tile // 2
        start = step * half
        shape = (half, 2, narrow, ch)
        gain = high_gain_ref[1:2]
        even = activate(high_conv(high_a, (2, 0, 3), start, tile, 0), gain)
        high_b[0, pl.ds(start, half)] = even.astype(BF16).reshape(shape)
        high_b[1, pl.ds(start, half)] = roll_up(even, 1).astype(BF16).reshape(shape)
        odd = activate(high_conv(high_a, (1, 2, 0), start, tile, 0), gain)
        high_b[2, pl.ds(start, half)] = odd.astype(BF16).reshape(shape)
        high_b[3, pl.ds(start, half)] = roll_up(odd, 1).astype(BF16).reshape(shape)

    last = high_b.shape[1] - 1

    @pl.when(at_top)
    def _():
        for k in range(4):
            high_b[k, 0, 0] = jnp.zeros((narrow, ch), BF16)

    @pl.when(at_bottom)
    def _():
        for k in range(4):
            high_b[k, last, 1] = jnp.zeros((narrow, ch), BF16)

    total = 2 * rows
    tile = tile_of(total, narrow, True)

    @pl.loop(0, total // tile)
    def _(step):
        half = tile // 2
        start = step * half
        shape = (tile, narrow, ch)
        for phase, slots in ((0, (2, 0, 3)), (1, (0, 3, 1))):
            summed = high_conv(high_b, slots, start, tile, 1)
            kept = field[phase, pl.ds(start + 1, half)].reshape(tile * narrow, ch)
            summed = (summed + kept.astype(F32)).reshape(tile * narrow, ch)
            summed = summed.reshape(shape)
            for lane in range(0, ch, 128):
                weave[lane // 128, :, pl.ds(phase, narrow, stride=2), :] = summed[
                    :, :, lane : lane + 128
                ]
        for lane in range(0, ch, 128):
            out_ref[pl.ds(2 * start, tile), :, lane : lane + 128] = weave[
                lane // 128, :, : 2 * cols, :
            ].astype(BF16)


def decode(band, patches, first, low_w, up_w, high_w, low_gain, high_gain, rows, cols, bands):
    pitch = patches.shape[1]
    ch = first.shape[1]
    narrow = round_up(cols + 1, 16)
    dims = (rows, cols, pitch, narrow, bands)
    vmem = pl.BlockSpec(memory_space=pltpu.VMEM)
    last_tile = tile_of(2 * rows, narrow, True)
    return pl.pallas_call(
        functools.partial(decoder_kernel, dims),
        out_shape=jax.ShapeDtypeStruct((2 * rows, 2 * cols, ch), BF16),
        in_specs=[pl.BlockSpec(memory_space=pltpu.SMEM)] + [vmem] * 7,
        out_specs=vmem,
        scratch_shapes=[
            pltpu.VMEM((rows + 8, pitch, ch), BF16),
            pltpu.VMEM((3, rows + 8, pitch, ch), BF16),
            pltpu.VMEM((3, rows + 6, pitch, ch), BF16),
            pltpu.VMEM((4, rows + 4, narrow, ch), BF16),
            pltpu.VMEM((2, 4 * ch, 2 * ch), BF16),
            pltpu.VMEM((2, rows + 2, 2, narrow, ch), BF16),
            pltpu.VMEM((4, rows + 2, 2, narrow, ch), BF16),
            pltpu.VMEM((4, rows + 1, 2, narrow, ch), BF16),
            pltpu.VMEM((ch // 128, last_tile, 2 * narrow, 128), F32),
        ],
        compiler_params=pltpu.CompilerParams(vmem_limit_bytes=56 * 1024 * 1024),
    )(band, patches, first, low_w, up_w, high_w, low_gain, high_gain)


def shards(
    denoised_tokens,
    sequence_row_index,
    latent_frame_cache,
    cache_slot_order,
    temporal_taps_weight,
    input_weight,
    latent_conv_weights,
    upsampled_weight,
    upper_conv_weights,
    latent_norm_gains,
    upper_norm_gains,
):
    sectors = lax.axis_size("lon")
    bands = lax.axis_size("band")
    rows = latent_frame_cache.shape[1]
    channels = temporal_taps_weight.shape[1]
    cols = latent_frame_cache.shape[2] // channels
    ch = input_weight.shape[2]
    edge = HALO * channels
    own = cols * channels
    wide = own + 2 * edge

    tokens = denoised_tokens.reshape(denoised_tokens.shape[1], denoised_tokens.shape[2])
    ring = jnp.concatenate([tokens[:, -edge:], tokens, tokens[:, :edge]], axis=1)
    windows = jnp.stack([ring[:, k * own : k * own + wide] for k in range(sectors)])
    arrived = lax.all_to_all(windows, "lon", split_axis=0, concat_axis=0, tiled=True)
    arrived = arrived.reshape(rows, wide)
    places = sequence_row_index[0][:, None] == jnp.arange(rows)[None, :]
    latent = jnp.dot(places.astype(BF16), arrived, preferred_element_type=F32).astype(BF16)

    frames = jnp.stack(
        [latent_frame_cache[cache_slot_order[0]], latent_frame_cache[cache_slot_order[1]]]
    )
    east = [(k, (k + 1) % sectors) for k in range(sectors)]
    west = [(target, source) for source, target in east]
    before = lax.ppermute(frames[:, :, -edge:], "lon", east)
    after = lax.ppermute(frames[:, :, :edge], "lon", west)
    frames = jnp.concatenate([before, frames, after], axis=2)
    stacked = jnp.concatenate([latent[None], frames], axis=0)
    south = [(k, k + 1) for k in range(bands - 1)]
    north = [(target, source) for source, target in south]
    above = lax.ppermute(stacked[:, -HALO:], "band", south)
    below = lax.ppermute(stacked[:, :HALO], "band", north)
    stacked = jnp.concatenate([above, stacked, below], axis=1)

    tall = rows + 2 * HALO
    span = cols + 2 * HALO
    cells = stacked.reshape(3, tall, span, channels).transpose(1, 2, 0, 3)
    cells = cells.reshape(tall * span, 3 * channels)
    taps = temporal_taps_weight.reshape(3 * channels, channels)
    temporal = jnp.dot(cells, taps, preferred_element_type=F32).astype(BF16)
    temporal = temporal.reshape(tall, span, channels)
    pitch = round_up(span, 16)
    temporal = jnp.pad(temporal, ((0, 0), (0, pitch + 2 - span), (0, 0)))
    patches = jnp.concatenate(
        [temporal[p : p + rows + 8, q : q + pitch] for p in range(3) for q in range(3)], axis=2
    )
    band = lax.axis_index("band").reshape(1).astype(jnp.int32)
    return decode(
        band,
        patches,
        input_weight.reshape(9 * channels, ch),
        latent_conv_weights.reshape(2, 9 * ch, ch),
        upsampled_weight,
        upper_conv_weights.reshape(2, 9 * ch, ch),
        latent_norm_gains,
        upper_norm_gains,
        rows,
        cols,
        bands,
    )


def solution(mesh):
    in_specs = (
        P("band", "lon", None),
        P("band", None),
        P(None, "band", "lon"),
        P(),
        P(),
        P(),
        P(),
        P(),
        P(),
        P(),
        P(),
    )
    out_specs = P("band", "lon", None)
    return jax.shard_map(shards, mesh=mesh, in_specs=in_specs, out_specs=out_specs, check_vma=False)
```

```python
import functools

import jax
import jax.numpy as jnp
from jax import lax
from jax.experimental import pallas as pl
from jax.experimental.pallas import tpu as pltpu
from jax.sharding import PartitionSpec as P

HALO = 5
LANES = 128
ROWS = 16
MESH = pl.DeviceIdType.MESH
F32 = jnp.float32
BF16 = jnp.bfloat16


def round_up(value, step):
    return (value + step - 1) // step * step


def tile_of(rows, pitch, even=False):
    best = 2 if even else 1
    for count in range(1, rows + 1):
        if rows % count == 0 and count * pitch <= 640 and not (even and count % 2):
            best = count
    return best


def activate(values, gain):
    scale = lax.rsqrt(jnp.mean(values * values, axis=-1, keepdims=True) + 1e-06)
    half = values * scale * (gain * 0.5)
    return half + half * jnp.tanh(half)


def roll_up(values, count):
    return pltpu.roll(values, values.shape[0] - count, 0)


def decoder_kernel(
    dims,
    band_ref,
    patches_ref,
    first_ref,
    low_w_ref,
    up_w_ref,
    high_w_ref,
    low_gain_ref,
    high_gain_ref,
    out_ref,
    opening,
    low_a,
    low_b,
    low_res,
    phase_w,
    field,
    high_a,
    high_b,
    weave,
):
    rows, cols, pitch, narrow, bands = dims
    ch = out_ref.shape[-1]
    band = band_ref[0]
    at_top = band == 0
    at_bottom = band == bands - 1

    def blank(ref, lead, row_slice):
        shape = ref.at[lead, row_slice].shape if lead is not None else ref.at[row_slice].shape
        if lead is None:
            ref[row_slice] = jnp.zeros(shape, ref.dtype)
        else:
            ref[lead, row_slice] = jnp.zeros(shape, ref.dtype)

    def blank_ends(ref, copies, top, bottom):
        total = ref.shape[1]

        @pl.when(at_top)
        def _():
            for k in range(copies):
                blank(ref, k, pl.ds(0, top))

        @pl.when(at_bottom)
        def _():
            for k in range(copies):
                blank(ref, k, pl.ds(total - bottom, bottom))

    total = rows + 8
    tile = tile_of(total, pitch)

    @pl.loop(0, total // tile)
    def _(step):
        start = step * tile
        part = patches_ref[pl.ds(start, tile)].reshape(tile * pitch, -1)
        summed = jnp.dot(part, first_ref[...], preferred_element_type=F32)
        summed = summed.astype(BF16).astype(F32)
        shape = (tile, pitch, ch)
        opening[pl.ds(start, tile)] = roll_up(summed, 2).astype(BF16).reshape(shape)
        active = activate(summed, low_gain_ref[0:1])
        low_a[0, pl.ds(start, tile)] = active.astype(BF16).reshape(shape)
        low_a[1, pl.ds(start, tile)] = roll_up(active, 1).astype(BF16).reshape(shape)
        low_a[2, pl.ds(start, tile)] = roll_up(active, 2).astype(BF16).reshape(shape)

    blank_ends(low_a, 3, 4, 4)

    def low_conv(source, start, tile, which):
        parts = []
        for p in range(3):
            for q in range(3):
                part = source[q, pl.ds(start + p, tile)]
                parts.append(part.reshape(tile * pitch, ch))
        return jnp.dot(
            jnp.concatenate(parts, axis=1), low_w_ref[which], preferred_element_type=F32
        )

    total = rows + 6
    tile = tile_of(total, pitch)

    @pl.loop(0, total // tile)
    def _(step):
        start = step * tile
        shape = (tile, pitch, ch)
        active = activate(low_conv(low_a, start, tile, 0), low_gain_ref[1:2])
        low_b[0, pl.ds(start, tile)] = active.astype(BF16).reshape(shape)
        low_b[1, pl.ds(start, tile)] = roll_up(active, 1).astype(BF16).reshape(shape)
        low_b[2, pl.ds(start, tile)] = roll_up(active, 2).astype(BF16).reshape(shape)

    blank_ends(low_b, 3, 3, 3)

    total = rows + 4
    tile = tile_of(total, pitch)

    @pl.loop(0, total // tile)
    def _(step):
        start = step * tile
        shape = (tile, pitch, ch)
        summed = low_conv(low_b, start, tile, 1)
        summed = summed + opening[pl.ds(start + 2, tile)].reshape(tile * pitch, ch).astype(F32)
        for shift in range(4):
            moved = summed if shift == 0 else roll_up(summed, shift)
            low_res[shift, pl.ds(start, tile)] = moved.astype(BF16).reshape(shape)[:, :narrow]

    blank_ends(low_res, 4, 2, 2)

    def tap(p, q):
        return up_w_ref[3 * p + q].astype(F32)

    groups = (((0,), (1, 2)), ((0, 1), (2,)))
    for a in range(2):
        for b in range(2):
            for p in range(2):
                for q in range(2):
                    summed = None
                    for pp in groups[a][p]:
                        for qq in groups[b][q]:
                            term = tap(pp, qq)
                            summed = term if summed is None else summed + term
                    base = (2 * p + q) * ch
                    phase_w[a, pl.ds(base, ch), pl.ds(b * ch, ch)] = summed.astype(BF16)

    total = rows + 2
    tile = tile_of(total, narrow)

    @pl.loop(0, total // tile)
    def _(step):
        start = step * tile
        shape = (tile, narrow, ch)
        for a in range(2):

            def up_conv(left, low_n, high_n):
                parts = []
                for p in range(2):
                    for q in range(2):
                        part = low_res[left + q, pl.ds(start + a + p, tile)]
                        parts.append(part.reshape(tile * narrow, ch))
                return jnp.dot(
                    jnp.concatenate(parts, axis=1),
                    phase_w[a, :, low_n:high_n],
                    preferred_element_type=F32,
                )

            def keep(slot, summed, kept):
                rounded = summed.astype(BF16)
                if kept is not None:
                    field[kept, pl.ds(start, tile), a] = rounded.reshape(shape)
                active = activate(rounded.astype(F32), high_gain_ref[0:1])
                high_a[slot, pl.ds(start, tile), a] = active.astype(BF16).reshape(shape)

            both = up_conv(1, 0, 2 * ch)
            keep(0, both[:, :ch], 0)
            keep(2, both[:, ch:], None)
            keep(1, up_conv(0, 0, ch), None)
            keep(3, up_conv(2, ch, 2 * ch), 1)

    blank_ends(high_a, 4, 1, 1)

    def high_conv(source, slots, start, tile, which):
        parts = []
        views = [
            source[s, pl.ds(start, tile // 2 + 1)].reshape(tile + 2, narrow, ch) for s in slots
        ]
        for p in range(3):
            for q in range(3):
                parts.append(views[q][p : p + tile].reshape(tile * narrow, ch))
        return jnp.dot(
            jnp.concatenate(parts, axis=1), high_w_ref[which], preferred_element_type=F32
        )

    total = 2 * rows + 2
    tile = tile_of(total, narrow, True)

    @pl.loop(0, total // tile)
    def _(step):
        half = tile // 2
        start = step * half
        shape = (half, 2, narrow, ch)
        gain = high_gain_ref[1:2]
        even = activate(high_conv(high_a, (2, 0, 3), start, tile, 0), gain)
        high_b[0, pl.ds(start, half)] = even.astype(BF16).reshape(shape)
        high_b[1, pl.ds(start, half)] = roll_up(even, 1).astype(BF16).reshape(shape)
        odd = activate(high_conv(high_a, (1, 2, 0), start, tile, 0), gain)
        high_b[2, pl.ds(start, half)] = odd.astype(BF16).reshape(shape)
        high_b[3, pl.ds(start, half)] = roll_up(odd, 1).astype(BF16).reshape(shape)

    last = high_b.shape[1] - 1

    @pl.when(at_top)
    def _():
        for k in range(4):
            high_b[k, 0, 0] = jnp.zeros((narrow, ch), BF16)

    @pl.when(at_bottom)
    def _():
        for k in range(4):
            high_b[k, last, 1] = jnp.zeros((narrow, ch), BF16)

    total = 2 * rows
    tile = tile_of(total, narrow, True)

    @pl.loop(0, total // tile)
    def _(step):
        half = tile // 2
        start = step * half
        shape = (tile, narrow, ch)
        for phase, slots in ((0, (2, 0, 3)), (1, (0, 3, 1))):
            summed = high_conv(high_b, slots, start, tile, 1)
            kept = field[phase, pl.ds(start + 1, half)].reshape(tile * narrow, ch)
            summed = (summed + kept.astype(F32)).reshape(tile * narrow, ch)
            summed = summed.reshape(shape)
            for lane in range(0, ch, 128):
                for t in range(tile):
                    spots = pl.ds(phase * total + 2 * start + t, narrow, stride=2 * total)
                    weave[lane // 128, spots, :] = summed[t, :, lane : lane + 128]

    for col in range(2 * cols):
        for lane in range(0, ch, 128):
            out_ref[col, :, lane : lane + 128] = weave[
                lane // 128, pl.ds(col * total, total), :
            ].astype(BF16)


def decode(band, patches, first, low_w, up_w, high_w, low_gain, high_gain, rows, cols, bands):
    pitch = patches.shape[1]
    ch = first.shape[1]
    narrow = round_up(cols + 1, 16)
    dims = (rows, cols, pitch, narrow, bands)
    vmem = pl.BlockSpec(memory_space=pltpu.VMEM)
    return pl.pallas_call(
        functools.partial(decoder_kernel, dims),
        out_shape=jax.ShapeDtypeStruct((2 * cols, 2 * rows, ch), BF16),
        in_specs=[pl.BlockSpec(memory_space=pltpu.SMEM)] + [vmem] * 7,
        out_specs=vmem,
        scratch_shapes=[
            pltpu.VMEM((rows + 8, pitch, ch), BF16),
            pltpu.VMEM((3, rows + 8, pitch, ch), BF16),
            pltpu.VMEM((3, rows + 6, pitch, ch), BF16),
            pltpu.VMEM((4, rows + 4, narrow, ch), BF16),
            pltpu.VMEM((2, 4 * ch, 2 * ch), BF16),
            pltpu.VMEM((2, rows + 2, 2, narrow, ch), BF16),
            pltpu.VMEM((4, rows + 2, 2, narrow, ch), BF16),
            pltpu.VMEM((4, rows + 1, 2, narrow, ch), BF16),
            pltpu.VMEM((ch // 128, 2 * narrow * 2 * rows, 128), F32),
        ],
        compiler_params=pltpu.CompilerParams(vmem_limit_bytes=56 * 1024 * 1024),
    )(band, patches, first, low_w, up_w, high_w, low_gain, high_gain)


def halo_kernel(
    dims, tokens_ref, places_ref, cache_ref, order_ref, arrived, places, frames, ring, *sems
):
    edge, sectors, bands, window = dims
    token_send, token_recv, place_send, place_recv, frame_send, frame_recv, own_sem = sems
    lon = lax.axis_index("lon")
    band = lax.axis_index("band")
    length = tokens_ref.shape[1]
    own = cache_ref.shape[2]
    rows = cache_ref.shape[1]
    broad = round_up(own, LANES)

    def sector(step):
        return lax.rem(lon + step + sectors, sectors)

    def inside(step):
        return jnp.logical_and(band + step >= 0, band + step < bands)

    def to(across, down):
        return {"lon": sector(across), "band": band + down}

    barrier = pltpu.get_barrier_semaphore()
    for down in (0, 1, -1):

        @pl.when(inside(down))
        def _():
            for across in range(sectors):
                if across or down:
                    pl.semaphore_signal(
                        barrier, inc=1, device_id=to(across, down), device_id_type=MESH
                    )

    ring[:, :LANES] = tokens_ref[:, length - LANES :]
    ring[:, LANES : LANES + length] = tokens_ref[...]
    ring[:, LANES + length :] = tokens_ref[:, : 2 * LANES]
    frames[:, ROWS : ROWS + rows, LANES : LANES + broad] = jnp.zeros(
        (2, rows, broad), frames.dtype
    )
    for k in range(2):
        frames[k, ROWS : ROWS + rows, LANES : LANES + own] = cache_ref[order_ref[k]]
    places[1] = places_ref[...]
    for slot, step, spot in ((0, -1, 0), (2, 1, ROWS + rows)):

        @pl.when(jnp.logical_not(inside(step)))
        def _():
            arrived[slot] = jnp.zeros(arrived.shape[1:], arrived.dtype)
            places[slot] = jnp.zeros(places.shape[1:], places.dtype)
            frames[:, spot : spot + ROWS] = jnp.zeros(
                (2, ROWS, frames.shape[2]), frames.dtype
            )

    neighbours = jnp.where(inside(-1), 1, 0) + jnp.where(inside(1), 1, 0) + 1
    pl.semaphore_wait(barrier, neighbours * sectors - 1)

    def token_copy(across, down, source):
        start = (sector(across) * own + LANES - edge) // LANES * LANES
        return pltpu.make_async_remote_copy(
            src_ref=ring.at[:, pl.ds(pl.multiple_of(start, LANES), window)],
            dst_ref=arrived.at[1 - down, source],
            send_sem=token_send.at[1 - down, across],
            recv_sem=token_recv.at[1 - down, across],
            device_id=to(across, down),
            device_id_type=MESH,
        )

    def place_copy(down):
        return pltpu.make_async_remote_copy(
            src_ref=places_ref,
            dst_ref=places.at[1 - down],
            send_sem=place_send.at[1 - down],
            recv_sem=place_recv.at[1 - down],
            device_id=to(0, down),
            device_id_type=MESH,
        )

    def frame_copy(across, down):
        tall = {0: (ROWS, ROWS, rows), 1: (rows, 0, ROWS), -1: (ROWS, ROWS + rows, ROWS)}[down]
        inner = LANES + (own - edge) // LANES * LANES
        flat = {
            0: (LANES, LANES, broad),
            1: (inner, 0, LANES),
            -1: (LANES, LANES + broad, LANES),
        }[across]
        return pltpu.make_async_remote_copy(
            src_ref=frames.at[:, pl.ds(tall[0], tall[2]), pl.ds(flat[0], flat[2])],
            dst_ref=frames.at[:, pl.ds(tall[1], tall[2]), pl.ds(flat[1], flat[2])],
            send_sem=frame_send.at[down + 1, across + 1],
            recv_sem=frame_recv.at[down + 1, across + 1],
            device_id=to(across, down),
            device_id_type=MESH,
        )

    mine = (lon * own + LANES - edge) // LANES * LANES
    stay = pltpu.make_async_copy(
        ring.at[:, pl.ds(pl.multiple_of(mine, LANES), window)], arrived.at[1, lon], own_sem
    )
    for down in (1, -1, 0):

        @pl.when(inside(down))
        def _():
            for across in range(sectors):
                if across or down:
                    token_copy(across, down, lon).start()
            for across in (-1, 0, 1):
                if across or down:
                    frame_copy(across, down).start()
            if down:
                place_copy(down).start()

    stay.start()
    for down in (0, 1, -1):

        @pl.when(inside(down))
        def _():
            for across in range(sectors):
                if across or down:
                    token_copy(across, down, lon).wait_send()
            for across in (-1, 0, 1):
                if across or down:
                    frame_copy(across, down).wait_send()
            if down:
                place_copy(down).wait_send()

        @pl.when(inside(-down))
        def _():
            for across in range(sectors):
                if across or down:
                    token_copy(across, down, sector(-across)).wait_recv()
            for across in (-1, 0, 1):
                if across or down:
                    frame_copy(across, down).wait_recv()
            if down:
                place_copy(down).wait_recv()

    stay.wait()


def gather_halos(tokens, places, cache, order, edge, sectors, bands):
    own = cache.shape[2]
    rows = cache.shape[1]
    window = round_up(own + 2 * edge + LANES - edge // HALO, LANES)
    vmem = pl.BlockSpec(memory_space=pltpu.VMEM)
    dma = pltpu.SemaphoreType.DMA
    return pl.pallas_call(
        functools.partial(halo_kernel, (edge, sectors, bands, window)),
        out_shape=[
            jax.ShapeDtypeStruct((3, sectors, tokens.shape[0], window), BF16),
            jax.ShapeDtypeStruct((3,) + places.shape, places.dtype),
            jax.ShapeDtypeStruct((2, rows + 2 * ROWS, round_up(own, LANES) + 2 * LANES), BF16),
        ],
        in_specs=[vmem, vmem, vmem, pl.BlockSpec(memory_space=pltpu.SMEM)],
        out_specs=[vmem] * 3,
        scratch_shapes=[
            pltpu.VMEM((tokens.shape[0], tokens.shape[1] + 3 * LANES), BF16),
            dma((3, sectors)),
            dma((3, sectors)),
            dma((3,)),
            dma((3,)),
            dma((3, 3)),
            dma((3, 3)),
            dma,
        ],
        compiler_params=pltpu.CompilerParams(collective_id=0, has_side_effects=True),
    )(tokens, places, cache, order)


def shards(
    denoised_tokens,
    sequence_row_index,
    latent_frame_cache,
    cache_slot_order,
    temporal_taps_weight,
    input_weight,
    latent_conv_weights,
    upsampled_weight,
    upper_conv_weights,
    latent_norm_gains,
    upper_norm_gains,
):
    sectors = lax.axis_size("lon")
    bands = lax.axis_size("band")
    rows = latent_frame_cache.shape[1]
    channels = temporal_taps_weight.shape[1]
    cols = latent_frame_cache.shape[2] // channels
    ch = input_weight.shape[2]
    edge = HALO * channels
    own = cols * channels
    wide = own + 2 * edge

    arrived, places, frames = gather_halos(
        denoised_tokens.reshape(denoised_tokens.shape[1:]),
        sequence_row_index,
        latent_frame_cache,
        cache_slot_order,
        edge,
        sectors,
        bands,
    )
    order = jnp.concatenate(
        [places[0, 0, -HALO:], places[1, 0] + rows, places[2, 0, :HALO] + 2 * rows]
    )
    chosen = (order[:, None] == jnp.arange(3 * rows)[None, :]).astype(BF16)
    arrived = arrived.reshape(3 * rows, arrived.shape[3])
    latent = jnp.dot(chosen, arrived, preferred_element_type=F32).astype(BF16)
    skew = lax.rem(lax.axis_index("lon") * own + LANES - edge, LANES)
    latent = lax.dynamic_slice_in_dim(latent, skew, wide, 1)
    inner = (own - edge) // LANES * LANES
    left = own - edge - inner
    broad = round_up(own, LANES)
    frames = frames[:, ROWS - HALO : ROWS + rows + HALO]
    frames = jnp.concatenate(
        [
            frames[:, :, left : left + edge],
            frames[:, :, LANES : LANES + own],
            frames[:, :, LANES + broad : LANES + broad + edge],
        ],
        axis=2,
    )
    stacked = jnp.concatenate([latent[None], frames], axis=0)

    tall = rows + 2 * HALO
    span = cols + 2 * HALO
    cells = stacked.reshape(3, tall, span, channels).transpose(1, 2, 0, 3)
    cells = cells.reshape(tall * span, 3 * channels)
    taps = temporal_taps_weight.reshape(3 * channels, channels)
    temporal = jnp.dot(cells, taps, preferred_element_type=F32).astype(BF16)
    temporal = temporal.reshape(tall, span, channels)
    pitch = round_up(span, 16)
    temporal = jnp.pad(temporal, ((0, 0), (0, pitch + 2 - span), (0, 0)))
    patches = jnp.concatenate(
        [temporal[p : p + rows + 8, q : q + pitch] for p in range(3) for q in range(3)], axis=2
    )
    band = lax.axis_index("band").reshape(1).astype(jnp.int32)
    decoded = decode(
        band,
        patches,
        input_weight.reshape(9 * channels, ch),
        latent_conv_weights.reshape(2, 9 * ch, ch),
        upsampled_weight,
        upper_conv_weights.reshape(2, 9 * ch, ch),
        latent_norm_gains,
        upper_norm_gains,
        rows,
        cols,
        bands,
    )
    return decoded.transpose(1, 0, 2)


def solution(mesh):
    in_specs = (
        P("band", "lon", None),
        P("band", None),
        P(None, "band", "lon"),
        P(),
        P(),
        P(),
        P(),
        P(),
        P(),
        P(),
        P(),
    )
    out_specs = P("band", "lon", None)
    return jax.shard_map(shards, mesh=mesh, in_specs=in_specs, out_specs=out_specs, check_vma=False)
```

```python
import functools

import jax
import jax.numpy as jnp
from jax import lax
from jax.experimental import pallas as pl
from jax.experimental.pallas import tpu as pltpu
from jax.sharding import PartitionSpec as P

HALO = 5
LANES = 128
ROWS = 16
MESH = pl.DeviceIdType.MESH
F32 = jnp.float32
BF16 = jnp.bfloat16


def round_up(value, step):
    return (value + step - 1) // step * step


def tile_of(rows, pitch, even=False):
    best = 2 if even else 1
    for count in range(1, rows + 1):
        if rows % count == 0 and count * pitch <= 640 and not (even and count % 2):
            best = count
    return best


def activate(values, gain):
    scale = lax.rsqrt(jnp.mean(values * values, axis=-1, keepdims=True) + 1e-06)
    half = values * scale * (gain * 0.5)
    return half + half * jnp.tanh(half)


def roll_up(values, count):
    return pltpu.roll(values, values.shape[0] - count, 0)


def decoder_kernel(
    dims,
    spot_ref,
    arrived_ref,
    places_ref,
    frames_ref,
    taps_ref,
    first_ref,
    low_hbm,
    up_hbm,
    high_hbm,
    low_gain_ref,
    high_gain_ref,
    out_ref,
    low_w_ref,
    up_w_ref,
    high_w_ref,
    weight_sems,
    sorted_rows,
    rim_rows,
    strip,
    first_w,
    fresh,
    opening,
    low_a,
    low_b,
    low_res,
    phase_w,
    field,
    high_a,
    high_b,
    weave,
):
    rows, cols, pitch, narrow, bands = dims
    ch = out_ref.shape[-1]
    band = spot_ref[0]
    at_top = band == 0
    at_bottom = band == bands - 1

    def blank(ref, lead, row_slice):
        shape = ref.at[lead, row_slice].shape if lead is not None else ref.at[row_slice].shape
        if lead is None:
            ref[row_slice] = jnp.zeros(shape, ref.dtype)
        else:
            ref[lead, row_slice] = jnp.zeros(shape, ref.dtype)

    def blank_ends(ref, copies, top, bottom):
        total = ref.shape[1]

        @pl.when(at_top)
        def _():
            for k in range(copies):
                blank(ref, k, pl.ds(0, top))

        @pl.when(at_bottom)
        def _():
            for k in range(copies):
                blank(ref, k, pl.ds(total - bottom, bottom))

    loads = [
        pltpu.make_async_copy(source, target, weight_sems.at[k])
        for k, (source, target) in enumerate(
            (
                (low_hbm.at[0], low_w_ref.at[0]),
                (low_hbm.at[1], low_w_ref.at[1]),
                (up_hbm, up_w_ref),
                (high_hbm.at[0], high_w_ref.at[0]),
                (high_hbm.at[1], high_w_ref.at[1]),
            )
        )
    ]
    for load in loads:
        load.start()

    window = arrived_ref.shape[3]
    held = arrived_ref.shape[2]
    channels = taps_ref.shape[1]
    edge = HALO * channels
    own = cols * channels
    broad = round_up(own, LANES)
    tall = round_up(rows + 2 * HALO, 16)
    for slot in range(3):
        for source in range(arrived_ref.shape[1]):
            at = slot * rows + source * held
            strip[at : at + held] = arrived_ref[slot, source].astype(F32)
    for slot in range(3):
        spots = jnp.broadcast_to(places_ref[slot], (rows, rows))
        hits = spots == lax.broadcasted_iota(jnp.int32, (rows, rows), 0)
        chosen = jnp.where(hits, 1.0, 0.0).T.astype(BF16)
        band_rows = strip[slot * rows : (slot + 1) * rows].astype(BF16)
        sorted_rows[slot * rows : (slot + 1) * rows] = jnp.dot(
            chosen, band_rows, preferred_element_type=F32
        )
    latent = sorted_rows[rows - HALO : rows - HALO + tall]
    sources = [pltpu.roll(latent, window - spot_ref[1], 1)]

    lanes = frames_ref.shape[2]
    inner = (own - edge) // LANES * LANES
    left = own - edge - inner
    lane = lax.broadcasted_iota(jnp.int32, (tall, lanes), 1)
    for k in range(2):
        rim_rows[...] = frames_ref[k].astype(F32)
        mosaic = rim_rows[ROWS - HALO : ROWS - HALO + tall]
        west = pltpu.roll(mosaic, lanes - left, 1) if left else mosaic
        middle = pltpu.roll(mosaic, lanes - (LANES - edge), 1)
        east = pltpu.roll(mosaic, lanes - (LANES + broad - edge - own), 1)
        sources.append(jnp.where(lane < edge, west, jnp.where(lane < edge + own, middle, east)))

    spread = lax.broadcasted_iota(jnp.int32, (LANES, channels), 0) % channels
    spread = spread == lax.broadcasted_iota(jnp.int32, (LANES, channels), 1)
    spread = jnp.where(spread, 1.0, 0.0).astype(BF16)
    gather = lax.broadcasted_iota(jnp.int32, (channels, LANES), 1) % channels
    gather = gather == lax.broadcasted_iota(jnp.int32, (channels, LANES), 0)
    gather = jnp.where(gather, 1.0, 0.0).astype(BF16)
    same = lax.broadcasted_iota(jnp.int32, (LANES, LANES), 0) // channels
    same = same == lax.broadcasted_iota(jnp.int32, (LANES, LANES), 1) // channels
    blocks = []
    for k in range(3):
        deep = jnp.dot(spread, taps_ref[k], preferred_element_type=F32).astype(BF16)
        deep = jnp.dot(deep, gather, preferred_element_type=F32)
        blocks.append(jnp.where(same, deep, 0.0).astype(BF16))
    blocks = jnp.concatenate(blocks, axis=0)
    span = round_up((cols + 2 * HALO) * channels, LANES)
    strip[tall : tall + 8, :span] = jnp.zeros((8, span), F32)
    for tile in range(0, span, LANES):
        mixed = jnp.concatenate([source[:, tile : tile + LANES] for source in sources], axis=1)
        temporal = jnp.dot(mixed.astype(BF16), blocks, preferred_element_type=F32)
        strip[:tall, tile : tile + LANES] = temporal.astype(BF16).astype(F32)

    deep = 3 * channels
    first_w[...] = jnp.zeros(first_w.shape, BF16)
    for p in range(3):
        first_w[p * LANES : p * LANES + deep] = first_ref[p * deep : (p + 1) * deep]
    shifted = [strip[p : p + tall, :span] for p in range(3)]
    group = 8
    for begin in range(0, cols + 8, group):
        stack = []
        columns = range(begin, min(begin + group, cols + 8))
        for col in columns:
            base = col * channels // LANES * LANES
            skew = col * channels - base
            pieces = []
            for p in range(3):
                if skew + deep <= LANES:
                    piece = shifted[p][:, base : base + LANES]
                    piece = pltpu.roll(piece, LANES - skew, 1) if skew else piece
                else:
                    piece = shifted[p][:, base : base + 2 * LANES]
                    piece = pltpu.roll(piece, 2 * LANES - skew, 1)[:, :LANES]
                pieces.append(piece.astype(BF16))
            stack.append(jnp.concatenate(pieces, axis=1))
        summed = jnp.dot(
            jnp.concatenate(stack, axis=0), first_w[...], preferred_element_type=F32
        )
        for k, col in enumerate(columns):
            for half in range(0, ch, LANES):
                fresh[half // LANES, pl.ds(col, rows + 8, stride=pitch), :] = summed[
                    k * tall : k * tall + rows + 8, half : half + LANES
                ]

    total = rows + 8
    tile = tile_of(total, pitch)

    @pl.loop(0, total // tile)
    def _(step):
        start = step * tile
        flat = pl.ds(pl.multiple_of(start * pitch, 16), tile * pitch)
        summed = jnp.concatenate([fresh[half, flat, :] for half in range(ch // LANES)], axis=1)
        summed = summed.astype(BF16).astype(F32)
        shape = (tile, pitch, ch)
        opening[pl.ds(start, tile)] = roll_up(summed, 2).astype(BF16).reshape(shape)
        active = activate(summed, low_gain_ref[0:1])
        low_a[0, pl.ds(start, tile)] = active.astype(BF16).reshape(shape)
        low_a[1, pl.ds(start, tile)] = roll_up(active, 1).astype(BF16).reshape(shape)
        low_a[2, pl.ds(start, tile)] = roll_up(active, 2).astype(BF16).reshape(shape)

    loads[0].wait()
    blank_ends(low_a, 3, 4, 4)

    def low_conv(source, start, tile, which):
        parts = []
        for p in range(3):
            for q in range(3):
                part = source[q, pl.ds(start + p, tile)]
                parts.append(part.reshape(tile * pitch, ch))
        return jnp.dot(
            jnp.concatenate(parts, axis=1), low_w_ref[which], preferred_element_type=F32
        )

    total = rows + 6
    tile = tile_of(total, pitch)

    @pl.loop(0, total // tile)
    def _(step):
        start = step * tile
        shape = (tile, pitch, ch)
        active = activate(low_conv(low_a, start, tile, 0), low_gain_ref[1:2])
        low_b[0, pl.ds(start, tile)] = active.astype(BF16).reshape(shape)
        low_b[1, pl.ds(start, tile)] = roll_up(active, 1).astype(BF16).reshape(shape)
        low_b[2, pl.ds(start, tile)] = roll_up(active, 2).astype(BF16).reshape(shape)

    blank_ends(low_b, 3, 3, 3)
    loads[1].wait()

    total = rows + 4
    tile = tile_of(total, pitch)

    @pl.loop(0, total // tile)
    def _(step):
        start = step * tile
        shape = (tile, pitch, ch)
        summed = low_conv(low_b, start, tile, 1)
        summed = summed + opening[pl.ds(start + 2, tile)].reshape(tile * pitch, ch).astype(F32)
        for shift in range(4):
            moved = summed if shift == 0 else roll_up(summed, shift)
            low_res[shift, pl.ds(start, tile)] = moved.astype(BF16).reshape(shape)[:, :narrow]

    blank_ends(low_res, 4, 2, 2)

    loads[2].wait()

    def tap(p, q):
        return up_w_ref[3 * p + q].astype(F32)

    groups = (((0,), (1, 2)), ((0, 1), (2,)))
    for a in range(2):
        for b in range(2):
            for p in range(2):
                for q in range(2):
                    summed = None
                    for pp in groups[a][p]:
                        for qq in groups[b][q]:
                            term = tap(pp, qq)
                            summed = term if summed is None else summed + term
                    base = (2 * p + q) * ch
                    phase_w[a, pl.ds(base, ch), pl.ds(b * ch, ch)] = summed.astype(BF16)

    total = rows + 2
    tile = tile_of(total, narrow)

    @pl.loop(0, total // tile)
    def _(step):
        start = step * tile
        shape = (tile, narrow, ch)
        for a in range(2):

            def up_conv(left, low_n, high_n):
                parts = []
                for p in range(2):
                    for q in range(2):
                        part = low_res[left + q, pl.ds(start + a + p, tile)]
                        parts.append(part.reshape(tile * narrow, ch))
                return jnp.dot(
                    jnp.concatenate(parts, axis=1),
                    phase_w[a, :, low_n:high_n],
                    preferred_element_type=F32,
                )

            def keep(slot, summed, kept):
                rounded = summed.astype(BF16)
                if kept is not None:
                    field[kept, pl.ds(start, tile), a] = rounded.reshape(shape)
                active = activate(rounded.astype(F32), high_gain_ref[0:1])
                high_a[slot, pl.ds(start, tile), a] = active.astype(BF16).reshape(shape)

            both = up_conv(1, 0, 2 * ch)
            keep(0, both[:, :ch], 0)
            keep(2, both[:, ch:], None)
            keep(1, up_conv(0, 0, ch), None)
            keep(3, up_conv(2, ch, 2 * ch), 1)

    blank_ends(high_a, 4, 1, 1)
    loads[3].wait()

    def high_conv(source, slots, start, tile, which):
        parts = []
        views = [
            source[s, pl.ds(start, tile // 2 + 1)].reshape(tile + 2, narrow, ch) for s in slots
        ]
        for p in range(3):
            for q in range(3):
                parts.append(views[q][p : p + tile].reshape(tile * narrow, ch))
        return jnp.dot(
            jnp.concatenate(parts, axis=1), high_w_ref[which], preferred_element_type=F32
        )

    total = 2 * rows + 2
    tile = tile_of(total, narrow, True)

    @pl.loop(0, total // tile)
    def _(step):
        half = tile // 2
        start = step * half
        shape = (half, 2, narrow, ch)
        gain = high_gain_ref[1:2]
        even = activate(high_conv(high_a, (2, 0, 3), start, tile, 0), gain)
        high_b[0, pl.ds(start, half)] = even.astype(BF16).reshape(shape)
        high_b[1, pl.ds(start, half)] = roll_up(even, 1).astype(BF16).reshape(shape)
        odd = activate(high_conv(high_a, (1, 2, 0), start, tile, 0), gain)
        high_b[2, pl.ds(start, half)] = odd.astype(BF16).reshape(shape)
        high_b[3, pl.ds(start, half)] = roll_up(odd, 1).astype(BF16).reshape(shape)

    last = high_b.shape[1] - 1

    @pl.when(at_top)
    def _():
        for k in range(4):
            high_b[k, 0, 0] = jnp.zeros((narrow, ch), BF16)

    @pl.when(at_bottom)
    def _():
        for k in range(4):
            high_b[k, last, 1] = jnp.zeros((narrow, ch), BF16)

    loads[4].wait()

    total = 2 * rows
    tile = tile_of(total, narrow, True)

    @pl.loop(0, total // tile)
    def _(step):
        half = tile // 2
        start = step * half
        shape = (tile, narrow, ch)
        for phase, slots in ((0, (2, 0, 3)), (1, (0, 3, 1))):
            summed = high_conv(high_b, slots, start, tile, 1)
            kept = field[phase, pl.ds(start + 1, half)].reshape(tile * narrow, ch)
            summed = (summed + kept.astype(F32)).reshape(tile * narrow, ch)
            summed = summed.reshape(shape)
            for lane in range(0, ch, 128):
                for t in range(tile):
                    spots = pl.ds(phase * total + 2 * start + t, narrow, stride=2 * total)
                    weave[lane // 128, spots, :] = summed[t, :, lane : lane + 128]

    for col in range(2 * cols):
        for lane in range(0, ch, 128):
            out_ref[col, :, lane : lane + 128] = weave[
                lane // 128, pl.ds(col * total, total), :
            ].astype(BF16)


def decode(spot, arrived, places, frames, taps, first, low_w, up_w, high_w, gains, dims):
    rows, cols, pitch, narrow, bands = dims
    ch = first.shape[1]
    window = arrived.shape[3]
    tall = round_up(rows + 2 * HALO, 16)
    vmem = pl.BlockSpec(memory_space=pltpu.VMEM)
    hbm = pl.BlockSpec(memory_space=pl.ANY)
    return pl.pallas_call(
        functools.partial(decoder_kernel, dims),
        out_shape=jax.ShapeDtypeStruct((2 * cols, 2 * rows, ch), BF16),
        in_specs=[pl.BlockSpec(memory_space=pltpu.SMEM)] + [vmem] * 5 + [hbm] * 3 + [vmem] * 2,
        out_specs=vmem,
        scratch_shapes=[
            pltpu.VMEM(low_w.shape, BF16),
            pltpu.VMEM(up_w.shape, BF16),
            pltpu.VMEM(high_w.shape, BF16),
            pltpu.SemaphoreType.DMA((5,)),
            pltpu.VMEM((3 * rows + tall, window), F32),
            pltpu.VMEM((rows + 2 * ROWS, frames.shape[2]), F32),
            pltpu.VMEM((max(3 * rows, tall + 8), window), F32),
            pltpu.VMEM((3 * LANES, ch), BF16),
            pltpu.VMEM((ch // LANES, (rows + 8) * pitch, LANES), F32),
            pltpu.VMEM((rows + 8, pitch, ch), BF16),
            pltpu.VMEM((3, rows + 8, pitch, ch), BF16),
            pltpu.VMEM((3, rows + 6, pitch, ch), BF16),
            pltpu.VMEM((4, rows + 4, narrow, ch), BF16),
            pltpu.VMEM((2, 4 * ch, 2 * ch), BF16),
            pltpu.VMEM((2, rows + 2, 2, narrow, ch), BF16),
            pltpu.VMEM((4, rows + 2, 2, narrow, ch), BF16),
            pltpu.VMEM((4, rows + 1, 2, narrow, ch), BF16),
            pltpu.VMEM((ch // LANES, 2 * narrow * 2 * rows, LANES), F32),
        ],
        compiler_params=pltpu.CompilerParams(vmem_limit_bytes=56 * 1024 * 1024),
    )(spot, arrived, places, frames, taps, first, low_w, up_w, high_w, *gains)


def halo_kernel(
    dims, tokens_ref, places_ref, cache_ref, order_ref, arrived, places, frames, ring, *sems
):
    edge, sectors, bands, window = dims
    token_send, token_recv, place_send, place_recv, frame_send, frame_recv, own_sem = sems
    lon = lax.axis_index("lon")
    band = lax.axis_index("band")
    length = tokens_ref.shape[1]
    own = cache_ref.shape[2]
    rows = cache_ref.shape[1]
    broad = round_up(own, LANES)

    def sector(step):
        return lax.rem(lon + step + sectors, sectors)

    def inside(step):
        return jnp.logical_and(band + step >= 0, band + step < bands)

    def to(across, down):
        return {"lon": sector(across), "band": band + down}

    barrier = pltpu.get_barrier_semaphore()
    for down in (0, 1, -1):

        @pl.when(inside(down))
        def _():
            for across in range(sectors):
                if across or down:
                    pl.semaphore_signal(
                        barrier, inc=1, device_id=to(across, down), device_id_type=MESH
                    )

    ring[:, :LANES] = tokens_ref[:, length - LANES :]
    ring[:, LANES : LANES + length] = tokens_ref[...]
    ring[:, LANES + length :] = tokens_ref[:, : 2 * LANES]
    frames[:, ROWS : ROWS + rows, LANES : LANES + broad] = jnp.zeros(
        (2, rows, broad), frames.dtype
    )
    for k in range(2):
        frames[k, ROWS : ROWS + rows, LANES : LANES + own] = cache_ref[order_ref[k]]
    places[1] = places_ref[...]
    for slot, step, spot in ((0, -1, 0), (2, 1, ROWS + rows)):

        @pl.when(jnp.logical_not(inside(step)))
        def _():
            arrived[slot] = jnp.zeros(arrived.shape[1:], arrived.dtype)
            places[slot] = jnp.zeros(places.shape[1:], places.dtype)
            frames[:, spot : spot + ROWS] = jnp.zeros(
                (2, ROWS, frames.shape[2]), frames.dtype
            )

    neighbours = jnp.where(inside(-1), 1, 0) + jnp.where(inside(1), 1, 0) + 1
    pl.semaphore_wait(barrier, neighbours * sectors - 1)

    def token_copy(across, down, source):
        start = (sector(across) * own + LANES - edge) // LANES * LANES
        return pltpu.make_async_remote_copy(
            src_ref=ring.at[:, pl.ds(pl.multiple_of(start, LANES), window)],
            dst_ref=arrived.at[1 - down, source],
            send_sem=token_send.at[1 - down, across],
            recv_sem=token_recv.at[1 - down, across],
            device_id=to(across, down),
            device_id_type=MESH,
        )

    def place_copy(down):
        return pltpu.make_async_remote_copy(
            src_ref=places_ref,
            dst_ref=places.at[1 - down],
            send_sem=place_send.at[1 - down],
            recv_sem=place_recv.at[1 - down],
            device_id=to(0, down),
            device_id_type=MESH,
        )

    def frame_copy(across, down):
        tall = {0: (ROWS, ROWS, rows), 1: (rows, 0, ROWS), -1: (ROWS, ROWS + rows, ROWS)}[down]
        inner = LANES + (own - edge) // LANES * LANES
        flat = {
            0: (LANES, LANES, broad),
            1: (inner, 0, LANES),
            -1: (LANES, LANES + broad, LANES),
        }[across]
        return pltpu.make_async_remote_copy(
            src_ref=frames.at[:, pl.ds(tall[0], tall[2]), pl.ds(flat[0], flat[2])],
            dst_ref=frames.at[:, pl.ds(tall[1], tall[2]), pl.ds(flat[1], flat[2])],
            send_sem=frame_send.at[down + 1, across + 1],
            recv_sem=frame_recv.at[down + 1, across + 1],
            device_id=to(across, down),
            device_id_type=MESH,
        )

    mine = (lon * own + LANES - edge) // LANES * LANES
    stay = pltpu.make_async_copy(
        ring.at[:, pl.ds(pl.multiple_of(mine, LANES), window)], arrived.at[1, lon], own_sem
    )
    for down in (1, -1, 0):

        @pl.when(inside(down))
        def _():
            for across in range(sectors):
                if across or down:
                    token_copy(across, down, lon).start()
            for across in (-1, 0, 1):
                if across or down:
                    frame_copy(across, down).start()
            if down:
                place_copy(down).start()

    stay.start()
    for down in (0, 1, -1):

        @pl.when(inside(down))
        def _():
            for across in range(sectors):
                if across or down:
                    token_copy(across, down, lon).wait_send()
            for across in (-1, 0, 1):
                if across or down:
                    frame_copy(across, down).wait_send()
            if down:
                place_copy(down).wait_send()

        @pl.when(inside(-down))
        def _():
            for across in range(sectors):
                if across or down:
                    token_copy(across, down, sector(-across)).wait_recv()
            for across in (-1, 0, 1):
                if across or down:
                    frame_copy(across, down).wait_recv()
            if down:
                place_copy(down).wait_recv()

    stay.wait()


def gather_halos(tokens, places, cache, order, edge, sectors, bands):
    own = cache.shape[2]
    rows = cache.shape[1]
    window = round_up(own + 2 * edge + LANES - edge // HALO, LANES)
    vmem = pl.BlockSpec(memory_space=pltpu.VMEM)
    dma = pltpu.SemaphoreType.DMA
    return pl.pallas_call(
        functools.partial(halo_kernel, (edge, sectors, bands, window)),
        out_shape=[
            jax.ShapeDtypeStruct((3, sectors, tokens.shape[0], window), BF16),
            jax.ShapeDtypeStruct((3,) + places.shape, places.dtype),
            jax.ShapeDtypeStruct((2, rows + 2 * ROWS, round_up(own, LANES) + 2 * LANES), BF16),
        ],
        in_specs=[vmem, vmem, vmem, pl.BlockSpec(memory_space=pltpu.SMEM)],
        out_specs=[vmem] * 3,
        scratch_shapes=[
            pltpu.VMEM((tokens.shape[0], tokens.shape[1] + 3 * LANES), BF16),
            dma((3, sectors)),
            dma((3, sectors)),
            dma((3,)),
            dma((3,)),
            dma((3, 3)),
            dma((3, 3)),
            dma,
        ],
        compiler_params=pltpu.CompilerParams(collective_id=0, has_side_effects=True),
    )(tokens, places, cache, order)


def shards(
    denoised_tokens,
    sequence_row_index,
    latent_frame_cache,
    cache_slot_order,
    temporal_taps_weight,
    input_weight,
    latent_conv_weights,
    upsampled_weight,
    upper_conv_weights,
    latent_norm_gains,
    upper_norm_gains,
):
    sectors = lax.axis_size("lon")
    bands = lax.axis_size("band")
    rows = latent_frame_cache.shape[1]
    channels = temporal_taps_weight.shape[1]
    cols = latent_frame_cache.shape[2] // channels
    ch = input_weight.shape[2]
    edge = HALO * channels
    own = cols * channels

    arrived, places, frames = gather_halos(
        denoised_tokens.reshape(denoised_tokens.shape[1:]),
        sequence_row_index,
        latent_frame_cache,
        cache_slot_order,
        edge,
        sectors,
        bands,
    )
    lon = lax.axis_index("lon")
    skew = lax.rem(lon * own + LANES - edge, LANES)
    spot = jnp.stack([lax.axis_index("band"), skew]).astype(jnp.int32)
    pitch = round_up(cols + 8, 16)
    narrow = round_up(cols + 1, 16)
    decoded = decode(
        spot,
        arrived,
        places,
        frames,
        temporal_taps_weight,
        input_weight.reshape(9 * channels, ch),
        latent_conv_weights.reshape(2, 9 * ch, ch),
        upsampled_weight,
        upper_conv_weights.reshape(2, 9 * ch, ch),
        (latent_norm_gains, upper_norm_gains),
        (rows, cols, pitch, narrow, bands),
    )
    return decoded.transpose(1, 0, 2)


def solution(mesh):
    in_specs = (
        P("band", "lon", None),
        P("band", None),
        P(None, "band", "lon"),
        P(),
        P(),
        P(),
        P(),
        P(),
        P(),
        P(),
        P(),
    )
    out_specs = P("band", "lon", None)
    return jax.shard_map(shards, mesh=mesh, in_specs=in_specs, out_specs=out_specs, check_vma=False)
```

```python
import functools

import jax
import jax.numpy as jnp
from jax import lax
from jax.experimental import pallas as pl
from jax.experimental.pallas import tpu as pltpu
from jax.sharding import PartitionSpec as P

HALO = 5
LANES = 128
ROWS = 16
MESH = pl.DeviceIdType.MESH
F32 = jnp.float32
BF16 = jnp.bfloat16


def round_up(value, step):
    return (value + step - 1) // step * step


def tile_of(rows, pitch, even=False):
    best = 2 if even else 1
    for count in range(1, rows + 1):
        if rows % count == 0 and count * pitch <= 640 and not (even and count % 2):
            best = count
    return best


def activate(values, gain):
    scale = lax.rsqrt(jnp.mean(values * values, axis=-1, keepdims=True) + 1e-06)
    half = values * scale * (gain * 0.5)
    return half + half * jnp.tanh(half)


def roll_up(values, count):
    return pltpu.roll(values, values.shape[0] - count, 0)


def decoder_kernel(
    dims,
    arrived_ref,
    places_ref,
    frames_ref,
    taps_ref,
    first_ref,
    low_hbm,
    up_hbm,
    high_hbm,
    low_gain_ref,
    high_gain_ref,
    out_ref,
    low_w_ref,
    up_w_ref,
    high_w_ref,
    weight_sems,
    sorted_rows,
    rim_rows,
    strip,
    first_w,
    fresh,
    opening,
    low_a,
    low_b,
    low_res,
    phase_w,
    field,
    high_a,
    high_b,
    weave,
):
    rows, cols, pitch, narrow, bands = dims
    ch = out_ref.shape[-1]
    band = lax.axis_index("band")
    at_top = band == 0
    at_bottom = band == bands - 1

    def blank(ref, lead, row_slice):
        shape = ref.at[lead, row_slice].shape if lead is not None else ref.at[row_slice].shape
        if lead is None:
            ref[row_slice] = jnp.zeros(shape, ref.dtype)
        else:
            ref[lead, row_slice] = jnp.zeros(shape, ref.dtype)

    def blank_ends(ref, copies, top, bottom):
        total = ref.shape[1]

        @pl.when(at_top)
        def _():
            for k in range(copies):
                blank(ref, k, pl.ds(0, top))

        @pl.when(at_bottom)
        def _():
            for k in range(copies):
                blank(ref, k, pl.ds(total - bottom, bottom))

    loads = [
        pltpu.make_async_copy(source, target, weight_sems.at[k])
        for k, (source, target) in enumerate(
            (
                (low_hbm.at[0], low_w_ref.at[0]),
                (low_hbm.at[1], low_w_ref.at[1]),
                (up_hbm, up_w_ref),
                (high_hbm.at[0], high_w_ref.at[0]),
                (high_hbm.at[1], high_w_ref.at[1]),
            )
        )
    ]
    for load in loads:
        load.start()

    window = arrived_ref.shape[3]
    held = arrived_ref.shape[2]
    channels = taps_ref.shape[1]
    edge = HALO * channels
    own = cols * channels
    broad = round_up(own, LANES)
    tall = round_up(rows + 2 * HALO, 16)
    for slot in range(3):
        for source in range(arrived_ref.shape[1]):
            at = slot * rows + source * held
            strip[at : at + held] = arrived_ref[slot, source].astype(F32)
    for slot in range(3):
        spots = jnp.broadcast_to(places_ref[slot], (rows, rows))
        hits = spots == lax.broadcasted_iota(jnp.int32, (rows, rows), 0)
        chosen = jnp.where(hits, 1.0, 0.0).T.astype(BF16)
        band_rows = strip[slot * rows : (slot + 1) * rows].astype(BF16)
        sorted_rows[slot * rows : (slot + 1) * rows] = jnp.dot(
            chosen, band_rows, preferred_element_type=F32
        )
    latent = sorted_rows[rows - HALO : rows - HALO + tall]
    skew = lax.rem(lax.axis_index("lon") * own + LANES - edge, LANES)
    sources = [pltpu.roll(latent, window - skew, 1)]

    lanes = frames_ref.shape[2]
    inner = (own - edge) // LANES * LANES
    left = own - edge - inner
    lane = lax.broadcasted_iota(jnp.int32, (tall, lanes), 1)
    for k in range(2):
        rim_rows[...] = frames_ref[k].astype(F32)
        mosaic = rim_rows[ROWS - HALO : ROWS - HALO + tall]
        west = pltpu.roll(mosaic, lanes - left, 1) if left else mosaic
        middle = pltpu.roll(mosaic, lanes - (LANES - edge), 1)
        east = pltpu.roll(mosaic, lanes - (LANES + broad - edge - own), 1)
        sources.append(jnp.where(lane < edge, west, jnp.where(lane < edge + own, middle, east)))

    spread = lax.broadcasted_iota(jnp.int32, (LANES, channels), 0) % channels
    spread = spread == lax.broadcasted_iota(jnp.int32, (LANES, channels), 1)
    spread = jnp.where(spread, 1.0, 0.0).astype(BF16)
    gather = lax.broadcasted_iota(jnp.int32, (channels, LANES), 1) % channels
    gather = gather == lax.broadcasted_iota(jnp.int32, (channels, LANES), 0)
    gather = jnp.where(gather, 1.0, 0.0).astype(BF16)
    same = lax.broadcasted_iota(jnp.int32, (LANES, LANES), 0) // channels
    same = same == lax.broadcasted_iota(jnp.int32, (LANES, LANES), 1) // channels
    blocks = []
    for k in range(3):
        deep = jnp.dot(spread, taps_ref[k], preferred_element_type=F32).astype(BF16)
        deep = jnp.dot(deep, gather, preferred_element_type=F32)
        blocks.append(jnp.where(same, deep, 0.0).astype(BF16))
    blocks = jnp.concatenate(blocks, axis=0)
    span = round_up((cols + 2 * HALO) * channels, LANES)
    strip[tall : tall + 8, :span] = jnp.zeros((8, span), F32)
    for tile in range(0, span, LANES):
        mixed = jnp.concatenate([source[:, tile : tile + LANES] for source in sources], axis=1)
        temporal = jnp.dot(mixed.astype(BF16), blocks, preferred_element_type=F32)
        strip[:tall, tile : tile + LANES] = temporal.astype(BF16).astype(F32)

    deep = 3 * channels
    first_w[...] = jnp.zeros(first_w.shape, BF16)
    for p in range(3):
        first_w[p * LANES : p * LANES + deep] = first_ref[p * deep : (p + 1) * deep]
    shifted = [strip[p : p + tall, :span] for p in range(3)]
    group = 8
    for begin in range(0, cols + 8, group):
        stack = []
        columns = range(begin, min(begin + group, cols + 8))
        for col in columns:
            base = col * channels // LANES * LANES
            skew = col * channels - base
            pieces = []
            for p in range(3):
                if skew + deep <= LANES:
                    piece = shifted[p][:, base : base + LANES]
                    piece = pltpu.roll(piece, LANES - skew, 1) if skew else piece
                else:
                    piece = shifted[p][:, base : base + 2 * LANES]
                    piece = pltpu.roll(piece, 2 * LANES - skew, 1)[:, :LANES]
                pieces.append(piece.astype(BF16))
            stack.append(jnp.concatenate(pieces, axis=1))
        summed = jnp.dot(
            jnp.concatenate(stack, axis=0), first_w[...], preferred_element_type=F32
        )
        for k, col in enumerate(columns):
            for half in range(0, ch, LANES):
                fresh[half // LANES, pl.ds(col, rows + 8, stride=pitch), :] = summed[
                    k * tall : k * tall + rows + 8, half : half + LANES
                ]

    total = rows + 8
    tile = tile_of(total, pitch)

    @pl.loop(0, total // tile, unroll=total // tile)
    def _(step):
        start = step * tile
        flat = pl.ds(pl.multiple_of(start * pitch, 16), tile * pitch)
        summed = jnp.concatenate([fresh[half, flat, :] for half in range(ch // LANES)], axis=1)
        summed = summed.astype(BF16).astype(F32)
        shape = (tile, pitch, ch)
        opening[pl.ds(start, tile)] = roll_up(summed, 2).astype(BF16).reshape(shape)
        active = activate(summed, low_gain_ref[0:1])
        low_a[0, pl.ds(start, tile)] = active.astype(BF16).reshape(shape)
        low_a[1, pl.ds(start, tile)] = roll_up(active, 1).astype(BF16).reshape(shape)
        low_a[2, pl.ds(start, tile)] = roll_up(active, 2).astype(BF16).reshape(shape)

    loads[0].wait()
    blank_ends(low_a, 3, 4, 4)

    def low_conv(source, start, tile, which):
        parts = []
        for p in range(3):
            for q in range(3):
                part = source[q, pl.ds(start + p, tile)]
                parts.append(part.reshape(tile * pitch, ch))
        return jnp.dot(
            jnp.concatenate(parts, axis=1), low_w_ref[which], preferred_element_type=F32
        )

    total = rows + 6
    tile = tile_of(total, pitch)

    @pl.loop(0, total // tile, unroll=total // tile)
    def _(step):
        start = step * tile
        shape = (tile, pitch, ch)
        active = activate(low_conv(low_a, start, tile, 0), low_gain_ref[1:2])
        low_b[0, pl.ds(start, tile)] = active.astype(BF16).reshape(shape)
        low_b[1, pl.ds(start, tile)] = roll_up(active, 1).astype(BF16).reshape(shape)
        low_b[2, pl.ds(start, tile)] = roll_up(active, 2).astype(BF16).reshape(shape)

    blank_ends(low_b, 3, 3, 3)
    loads[1].wait()

    total = rows + 4
    tile = tile_of(total, pitch)

    @pl.loop(0, total // tile, unroll=total // tile)
    def _(step):
        start = step * tile
        shape = (tile, pitch, ch)
        summed = low_conv(low_b, start, tile, 1)
        summed = summed + opening[pl.ds(start + 2, tile)].reshape(tile * pitch, ch).astype(F32)
        for shift in range(4):
            moved = summed if shift == 0 else roll_up(summed, shift)
            low_res[shift, pl.ds(start, tile)] = moved.astype(BF16).reshape(shape)[:, :narrow]

    blank_ends(low_res, 4, 2, 2)

    loads[2].wait()

    def tap(p, q):
        return up_w_ref[3 * p + q].astype(F32)

    groups = (((0,), (1, 2)), ((0, 1), (2,)))
    for a in range(2):
        for b in range(2):
            for p in range(2):
                for q in range(2):
                    summed = None
                    for pp in groups[a][p]:
                        for qq in groups[b][q]:
                            term = tap(pp, qq)
                            summed = term if summed is None else summed + term
                    base = (2 * p + q) * ch
                    phase_w[a, pl.ds(base, ch), pl.ds(b * ch, ch)] = summed.astype(BF16)

    total = rows + 2
    tile = tile_of(total, narrow)

    @pl.loop(0, total // tile, unroll=total // tile)
    def _(step):
        start = step * tile
        shape = (tile, narrow, ch)
        for a in range(2):

            def up_conv(left, low_n, high_n):
                parts = []
                for p in range(2):
                    for q in range(2):
                        part = low_res[left + q, pl.ds(start + a + p, tile)]
                        parts.append(part.reshape(tile * narrow, ch))
                return jnp.dot(
                    jnp.concatenate(parts, axis=1),
                    phase_w[a, :, low_n:high_n],
                    preferred_element_type=F32,
                )

            def keep(slot, summed, kept):
                rounded = summed.astype(BF16)
                if kept is not None:
                    field[kept, pl.ds(start, tile), a] = rounded.reshape(shape)
                active = activate(rounded.astype(F32), high_gain_ref[0:1])
                high_a[slot, pl.ds(start, tile), a] = active.astype(BF16).reshape(shape)

            both = up_conv(1, 0, 2 * ch)
            keep(0, both[:, :ch], 0)
            keep(2, both[:, ch:], None)
            keep(1, up_conv(0, 0, ch), None)
            keep(3, up_conv(2, ch, 2 * ch), 1)

    blank_ends(high_a, 4, 1, 1)
    loads[3].wait()

    def high_conv(source, slots, start, tile, which):
        parts = []
        views = [
            source[s, pl.ds(start, tile // 2 + 1)].reshape(tile + 2, narrow, ch) for s in slots
        ]
        for p in range(3):
            for q in range(3):
                parts.append(views[q][p : p + tile].reshape(tile * narrow, ch))
        return jnp.dot(
            jnp.concatenate(parts, axis=1), high_w_ref[which], preferred_element_type=F32
        )

    total = 2 * rows + 2
    tile = tile_of(total, narrow, True)

    @pl.loop(0, total // tile, unroll=total // tile)
    def _(step):
        half = tile // 2
        start = step * half
        shape = (half, 2, narrow, ch)
        gain = high_gain_ref[1:2]
        even = activate(high_conv(high_a, (2, 0, 3), start, tile, 0), gain)
        high_b[0, pl.ds(start, half)] = even.astype(BF16).reshape(shape)
        high_b[1, pl.ds(start, half)] = roll_up(even, 1).astype(BF16).reshape(shape)
        odd = activate(high_conv(high_a, (1, 2, 0), start, tile, 0), gain)
        high_b[2, pl.ds(start, half)] = odd.astype(BF16).reshape(shape)
        high_b[3, pl.ds(start, half)] = roll_up(odd, 1).astype(BF16).reshape(shape)

    last = high_b.shape[1] - 1

    @pl.when(at_top)
    def _():
        for k in range(4):
            high_b[k, 0, 0] = jnp.zeros((narrow, ch), BF16)

    @pl.when(at_bottom)
    def _():
        for k in range(4):
            high_b[k, last, 1] = jnp.zeros((narrow, ch), BF16)

    loads[4].wait()

    total = 2 * rows
    tile = tile_of(total, narrow, True)

    @pl.loop(0, total // tile, unroll=total // tile)
    def _(step):
        half = tile // 2
        start = step * half
        shape = (tile, narrow, ch)
        for phase, slots in ((0, (2, 0, 3)), (1, (0, 3, 1))):
            summed = high_conv(high_b, slots, start, tile, 1)
            kept = field[phase, pl.ds(start + 1, half)].reshape(tile * narrow, ch)
            summed = (summed + kept.astype(F32)).reshape(tile * narrow, ch)
            summed = summed.reshape(shape)
            for lane in range(0, ch, 128):
                for t in range(tile):
                    spots = pl.ds(phase * total + 2 * start + t, narrow, stride=2 * total)
                    weave[lane // 128, spots, :] = summed[t, :, lane : lane + 128]

    for col in range(2 * cols):
        for lane in range(0, ch, 128):
            out_ref[col, :, lane : lane + 128] = weave[
                lane // 128, pl.ds(col * total, total), :
            ].astype(BF16)


def decode(arrived, places, frames, taps, first, low_w, up_w, high_w, gains, dims):
    rows, cols, pitch, narrow, bands = dims
    ch = first.shape[1]
    window = arrived.shape[3]
    tall = round_up(rows + 2 * HALO, 16)
    vmem = pl.BlockSpec(memory_space=pltpu.VMEM)
    hbm = pl.BlockSpec(memory_space=pl.ANY)
    return pl.pallas_call(
        functools.partial(decoder_kernel, dims),
        out_shape=jax.ShapeDtypeStruct((2 * cols, 2 * rows, ch), BF16),
        in_specs=[vmem] * 5 + [hbm] * 3 + [vmem] * 2,
        out_specs=vmem,
        scratch_shapes=[
            pltpu.VMEM(low_w.shape, BF16),
            pltpu.VMEM(up_w.shape, BF16),
            pltpu.VMEM(high_w.shape, BF16),
            pltpu.SemaphoreType.DMA((5,)),
            pltpu.VMEM((3 * rows + tall, window), F32),
            pltpu.VMEM((rows + 2 * ROWS, frames.shape[2]), F32),
            pltpu.VMEM((max(3 * rows, tall + 8), window), F32),
            pltpu.VMEM((3 * LANES, ch), BF16),
            pltpu.VMEM((ch // LANES, (rows + 8) * pitch, LANES), F32),
            pltpu.VMEM((rows + 8, pitch, ch), BF16),
            pltpu.VMEM((3, rows + 8, pitch, ch), BF16),
            pltpu.VMEM((3, rows + 6, pitch, ch), BF16),
            pltpu.VMEM((4, rows + 4, narrow, ch), BF16),
            pltpu.VMEM((2, 4 * ch, 2 * ch), BF16),
            pltpu.VMEM((2, rows + 2, 2, narrow, ch), BF16),
            pltpu.VMEM((4, rows + 2, 2, narrow, ch), BF16),
            pltpu.VMEM((4, rows + 1, 2, narrow, ch), BF16),
            pltpu.VMEM((ch // LANES, 2 * narrow * 2 * rows, LANES), F32),
        ],
        compiler_params=pltpu.CompilerParams(vmem_limit_bytes=56 * 1024 * 1024),
    )(arrived, places, frames, taps, first, low_w, up_w, high_w, *gains)


def halo_kernel(
    dims, tokens_ref, places_ref, cache_ref, order_ref, arrived, places, frames, ring, *sems
):
    edge, sectors, bands, window = dims
    token_send, token_recv, place_send, place_recv, frame_send, frame_recv, own_sem = sems
    lon = lax.axis_index("lon")
    band = lax.axis_index("band")
    length = tokens_ref.shape[1]
    own = cache_ref.shape[2]
    rows = cache_ref.shape[1]
    broad = round_up(own, LANES)

    def sector(step):
        return lax.rem(lon + step + sectors, sectors)

    def inside(step):
        return jnp.logical_and(band + step >= 0, band + step < bands)

    def to(across, down):
        return {"lon": sector(across), "band": band + down}

    barrier = pltpu.get_barrier_semaphore()
    for down in (0, 1, -1):

        @pl.when(inside(down))
        def _():
            for across in range(sectors):
                if across or down:
                    pl.semaphore_signal(
                        barrier, inc=1, device_id=to(across, down), device_id_type=MESH
                    )

    ring[:, :LANES] = tokens_ref[:, length - LANES :]
    ring[:, LANES : LANES + length] = tokens_ref[...]
    ring[:, LANES + length :] = tokens_ref[:, : 2 * LANES]
    frames[:, ROWS : ROWS + rows, LANES : LANES + broad] = jnp.zeros(
        (2, rows, broad), frames.dtype
    )
    for k in range(2):
        frames[k, ROWS : ROWS + rows, LANES : LANES + own] = cache_ref[order_ref[k]]
    places[1] = places_ref[...]
    for slot, step, spot in ((0, -1, 0), (2, 1, ROWS + rows)):

        @pl.when(jnp.logical_not(inside(step)))
        def _():
            arrived[slot] = jnp.zeros(arrived.shape[1:], arrived.dtype)
            places[slot] = jnp.zeros(places.shape[1:], places.dtype)
            frames[:, spot : spot + ROWS] = jnp.zeros(
                (2, ROWS, frames.shape[2]), frames.dtype
            )

    neighbours = jnp.where(inside(-1), 1, 0) + jnp.where(inside(1), 1, 0) + 1
    pl.semaphore_wait(barrier, neighbours * sectors - 1)

    def token_copy(across, down, source):
        start = (sector(across) * own + LANES - edge) // LANES * LANES
        return pltpu.make_async_remote_copy(
            src_ref=ring.at[:, pl.ds(pl.multiple_of(start, LANES), window)],
            dst_ref=arrived.at[1 - down, source],
            send_sem=token_send.at[1 - down, across],
            recv_sem=token_recv.at[1 - down, across],
            device_id=to(across, down),
            device_id_type=MESH,
        )

    def place_copy(down):
        return pltpu.make_async_remote_copy(
            src_ref=places_ref,
            dst_ref=places.at[1 - down],
            send_sem=place_send.at[1 - down],
            recv_sem=place_recv.at[1 - down],
            device_id=to(0, down),
            device_id_type=MESH,
        )

    def frame_copy(across, down):
        tall = {0: (ROWS, ROWS, rows), 1: (rows, 0, ROWS), -1: (ROWS, ROWS + rows, ROWS)}[down]
        inner = LANES + (own - edge) // LANES * LANES
        flat = {
            0: (LANES, LANES, broad),
            1: (inner, 0, LANES),
            -1: (LANES, LANES + broad, LANES),
        }[across]
        return pltpu.make_async_remote_copy(
            src_ref=frames.at[:, pl.ds(tall[0], tall[2]), pl.ds(flat[0], flat[2])],
            dst_ref=frames.at[:, pl.ds(tall[1], tall[2]), pl.ds(flat[1], flat[2])],
            send_sem=frame_send.at[down + 1, across + 1],
            recv_sem=frame_recv.at[down + 1, across + 1],
            device_id=to(across, down),
            device_id_type=MESH,
        )

    mine = (lon * own + LANES - edge) // LANES * LANES
    stay = pltpu.make_async_copy(
        ring.at[:, pl.ds(pl.multiple_of(mine, LANES), window)], arrived.at[1, lon], own_sem
    )
    for down in (1, -1, 0):

        @pl.when(inside(down))
        def _():
            for across in range(sectors):
                if across or down:
                    token_copy(across, down, lon).start()
            for across in (-1, 0, 1):
                if across or down:
                    frame_copy(across, down).start()
            if down:
                place_copy(down).start()

    stay.start()
    for down in (0, 1, -1):

        @pl.when(inside(down))
        def _():
            for across in range(sectors):
                if across or down:
                    token_copy(across, down, lon).wait_send()
            for across in (-1, 0, 1):
                if across or down:
                    frame_copy(across, down).wait_send()
            if down:
                place_copy(down).wait_send()

        @pl.when(inside(-down))
        def _():
            for across in range(sectors):
                if across or down:
                    token_copy(across, down, sector(-across)).wait_recv()
            for across in (-1, 0, 1):
                if across or down:
                    frame_copy(across, down).wait_recv()
            if down:
                place_copy(down).wait_recv()

    stay.wait()


def gather_halos(tokens, places, cache, order, edge, sectors, bands):
    own = cache.shape[2]
    rows = cache.shape[1]
    window = round_up(own + 2 * edge + LANES - edge // HALO, LANES)
    vmem = pl.BlockSpec(memory_space=pltpu.VMEM)
    dma = pltpu.SemaphoreType.DMA
    return pl.pallas_call(
        functools.partial(halo_kernel, (edge, sectors, bands, window)),
        out_shape=[
            jax.ShapeDtypeStruct((3, sectors, tokens.shape[0], window), BF16),
            jax.ShapeDtypeStruct((3,) + places.shape, places.dtype),
            jax.ShapeDtypeStruct((2, rows + 2 * ROWS, round_up(own, LANES) + 2 * LANES), BF16),
        ],
        in_specs=[vmem, vmem, vmem, pl.BlockSpec(memory_space=pltpu.SMEM)],
        out_specs=[vmem] * 3,
        scratch_shapes=[
            pltpu.VMEM((tokens.shape[0], tokens.shape[1] + 3 * LANES), BF16),
            dma((3, sectors)),
            dma((3, sectors)),
            dma((3,)),
            dma((3,)),
            dma((3, 3)),
            dma((3, 3)),
            dma,
        ],
        compiler_params=pltpu.CompilerParams(collective_id=0, has_side_effects=True),
    )(tokens, places, cache, order)


def shards(
    denoised_tokens,
    sequence_row_index,
    latent_frame_cache,
    cache_slot_order,
    temporal_taps_weight,
    input_weight,
    latent_conv_weights,
    upsampled_weight,
    upper_conv_weights,
    latent_norm_gains,
    upper_norm_gains,
):
    sectors = lax.axis_size("lon")
    bands = lax.axis_size("band")
    rows = latent_frame_cache.shape[1]
    channels = temporal_taps_weight.shape[1]
    cols = latent_frame_cache.shape[2] // channels
    ch = input_weight.shape[2]
    edge = HALO * channels
    own = cols * channels

    arrived, places, frames = gather_halos(
        denoised_tokens.reshape(denoised_tokens.shape[1:]),
        sequence_row_index,
        latent_frame_cache,
        cache_slot_order,
        edge,
        sectors,
        bands,
    )
    pitch = round_up(cols + 8, 16)
    narrow = round_up(cols + 1, 16)
    decoded = decode(
        arrived,
        places,
        frames,
        temporal_taps_weight,
        input_weight.reshape(9 * channels, ch),
        latent_conv_weights.reshape(2, 9 * ch, ch),
        upsampled_weight,
        upper_conv_weights.reshape(2, 9 * ch, ch),
        (latent_norm_gains, upper_norm_gains),
        (rows, cols, pitch, narrow, bands),
    )
    return decoded.transpose(1, 0, 2)


def solution(mesh):
    in_specs = (
        P("band", "lon", None),
        P("band", None),
        P(None, "band", "lon"),
        P(),
        P(),
        P(),
        P(),
        P(),
        P(),
        P(),
        P(),
    )
    out_specs = P("band", "lon", None)
    return jax.shard_map(shards, mesh=mesh, in_specs=in_specs, out_specs=out_specs, check_vma=False)
```
